512 devices in a mesh: grp: 2 (over x_lo), gene: 4 (over x_hi, core), cell: 64 (over z, y).
Axes of the slice: x: 4 (x_hi: 2, x_lo: 2; x = x_hi * 2 + x_lo), y: 8, z: 8, core: 2. Of those that a mesh axis runs over, the one named last changes fastest.
Arguments:
- data: bfloat16 [2, 15360, 16384], P('grp', 'gene', 'cell'), may hold values from 0 to 48
- shared_w: float32 [15360, 256], P(('gene', 'cell')), may hold values from 0.002 to 2
- specific_v: float32 [2, 15360, 256], P('grp', ('gene', 'cell')), may hold values from 0.0005 to 0.5
- factor_h: float32 [2, 256, 16384], P('grp', None, 'cell'), may hold values from 0.01 to 1
- cell_count: int32 [2], P('grp'), may hold values from 4096 to 16384, as said below
Outputs:
- new_w: float32 [15360, 256], P(('gene', 'cell'))
- new_v: float32 [2, 15360, 256], P('grp', ('gene', 'cell'))
- new_h: float32 [2, 256, 16384], P('grp', None, 'cell')
The draws below stay inside these ranges and needn't reach their ends.
Inputs may be any that keep to these rules, and one draw needn't show every extreme that they name: `cell_count`: in each draw one dataset, chosen from the seed, has all 16384 cell slots live and the other between 4096 and 8192; the live slots are the first ones.
All inputs are finite; a program needn't handle non-finite values.
Results may differ from the reference program's by a relative error of at most 0.0044.
Values may be sent and summed in bfloat16 or wider, within the bound.
A program may use at most 64 MiB of HBM per device.

```python
import math
import jax
import jax.numpy as jnp
from jax import lax

G = 15360
K = 256
KB = 32
SWEEPS = 4
NC = 16384


def draw_cell_count(key, part):
    first, second = jax.random.split(jax.random.fold_in(key, 17))
    small = jax.random.randint(first, (), NC // 4, NC // 2 + 1, dtype=jnp.int32)
    which = jax.random.randint(second, (), 0, 2, dtype=jnp.int32)
    full = jnp.full((), NC, jnp.int32)
    return jnp.stack([jnp.where(which == 0, full, small), jnp.where(which == 0, small, full)])


def level_of(stream_key, dims, shards, least, top_value):
    factor_of, own = 1.0, jax.random.fold_in(stream_key, 6)
    for dim, shards_of in shards:
        steps = jnp.exp(jax.random.uniform(jax.random.fold_in(own, dim), (shards_of,), jnp.float32, least / len(shards), top_value / len(shards)))
        factor_of = factor_of * jnp.repeat(steps, dims[dim] // shards_of).reshape([-1 if axis == dim else 1 for axis in range(len(dims))])
    return factor_of


def setup_inputs(seed: int = 0) -> dict:
    key_of = jax.random.split(jax.random.key(seed), 6)
    return {
        "data": jnp.clip(48.0 * jax.random.uniform(key_of[0], (2, G, NC), jnp.float32) ** level_of(key_of[0], (2, G, NC), ((0, 2), (1, 4), (2, 64)), -0.2, 0.2), 0.0, 48.0).astype(jnp.bfloat16),
        "shared_w": jnp.clip(jnp.exp(math.log(2.0) - 6.9077552 * jax.random.uniform(key_of[1], (G, K), jnp.float32) ** level_of(key_of[1], (G, K), ((0, 256),), -0.2, 0.2)), 0.002, 2.0),
        "specific_v": jnp.clip(jnp.exp(math.log(0.5) - 6.9077552 * jax.random.uniform(key_of[2], (2, G, K), jnp.float32) ** level_of(key_of[2], (2, G, K), ((0, 2), (1, 256)), -0.2, 0.2)), 0.0005, 0.5),
        "factor_h": jnp.clip(jnp.exp(math.log(1.0) - 4.6051702 * jax.random.uniform(key_of[3], (2, K, NC), jnp.float32) ** level_of(key_of[3], (2, K, NC), ((0, 2), (2, 64)), -0.2, 0.2)), 0.01, 1.0),
        "cell_count": draw_cell_count(jax.random.fold_in(key_of[5], 71), 0),
    }


LAMBDA = 5.0
TINY = 1e-6
HIGH = lax.Precision.HIGHEST


def sweep_rows(state, gram, drive, live, width):
    def one(index, state):
        start = jnp.asarray(index).astype(jnp.int32) * width
        rows = lax.dynamic_slice_in_dim(gram, start, width, 0)
        grad = jnp.dot(rows, state, precision=HIGH) - lax.dynamic_slice_in_dim(drive, start, width, 0)
        block = lax.dynamic_slice_in_dim(rows, start, width, 1)
        scale = jnp.sum(jnp.abs(block), axis=1) + TINY
        current = lax.dynamic_slice_in_dim(state, start, width, 0)
        fresh = jnp.maximum(current - grad / scale[:, None], 0.0) * live[None, :]
        return lax.dynamic_update_slice_in_dim(state, fresh, start, 0)
    for sweep in range(SWEEPS):
        state = lax.fori_loop(0, K // width, one, state)
    return state


def sweep_columns(matrix, offset, quad, target, factor, width):
    def one(index, matrix):
        start = jnp.asarray(index).astype(jnp.int32) * width
        cols = lax.dynamic_slice_in_dim(quad, start, width, 1)
        grad = jnp.dot(factor * matrix + offset, cols, precision=HIGH) - lax.dynamic_slice_in_dim(target, start, width, 1)
        block = lax.dynamic_slice_in_dim(cols, start, width, 0)
        scale = factor * jnp.sum(jnp.abs(block), axis=0) + TINY
        current = lax.dynamic_slice_in_dim(matrix, start, width, 1)
        fresh = jnp.maximum(current - grad / scale[None, :], 0.0)
        return lax.dynamic_update_slice_in_dim(matrix, fresh, start, 1)
    for sweep in range(SWEEPS):
        matrix = lax.fori_loop(0, K // width, one, matrix)
    return matrix


def reference(data, shared_w, specific_v, factor_h, cell_count):
    slots = jnp.arange(NC, dtype=jnp.int32)
    new_v = []
    new_h = []
    rest = jnp.zeros(shared_w.shape, jnp.float32)
    cross_sum = jnp.zeros((K, K), jnp.float32)
    for group in range(2):
        expr = data[group]
        mix = (shared_w + specific_v[group]).astype(jnp.bfloat16)
        own = specific_v[group].astype(jnp.bfloat16)
        gram = jnp.dot(mix.T, mix, preferred_element_type=jnp.float32) + LAMBDA * jnp.dot(own.T, own, preferred_element_type=jnp.float32)
        drive = jnp.dot(mix.T, expr, preferred_element_type=jnp.float32)
        live = (slots < cell_count[group]).astype(jnp.float32)
        state = sweep_rows(factor_h[group], gram, drive, live, KB)
        rounded = state.astype(jnp.bfloat16)
        proj = jnp.dot(expr, rounded.T, preferred_element_type=jnp.float32)
        cross = jnp.dot(rounded, rounded.T, preferred_element_type=jnp.float32)
        loading = sweep_columns(specific_v[group], shared_w, cross, proj, 1.0 + LAMBDA, KB)
        rest = rest + proj - jnp.dot(loading, cross, precision=HIGH)
        cross_sum = cross_sum + cross
        new_v.append(loading)
        new_h.append(state)
    new_w = sweep_columns(shared_w, jnp.zeros(shared_w.shape, jnp.float32), cross_sum, rest, 1.0, KB)
    return new_w, jnp.stack(new_v), jnp.stack(new_h)
```

```python
import jax
import jax.numpy as jnp
from jax import lax
from jax.experimental import pallas as pl
from jax.experimental.pallas import tpu as pltpu
from jax.sharding import PartitionSpec as P

K = 256
KB = 32
SWEEPS = 4
LAMBDA = 5.0
TINY = 1e-06
N = 8
GENES = 4
OWN = 60
ROWS = 64
HALF = 32
F32 = jnp.float32
BF16 = jnp.bfloat16
MESH = pl.DeviceIdType.MESH


def dot(left, right, left_dim=1, right_dim=0):
    return lax.dot_general(
        left, right, (((left_dim,), (right_dim,)), ((), ())), preferred_element_type=F32
    )


def split(x):
    high = x.astype(BF16)
    return high, (x - high.astype(F32)).astype(BF16)


def dot_split(left, high, low):
    one, two = split(left)
    return dot(one, high) + (dot(two, high) + dot(one, low))


def block_scale(quad):
    row = lax.broadcasted_iota(jnp.int32, (K, K), 0) // KB
    col = lax.broadcasted_iota(jnp.int32, (K, K), 1) // KB
    return jnp.sum(jnp.where(row == col, jnp.abs(quad), 0.0), axis=0, keepdims=True)


def sweeps(state, resid, quads, inverse, factor, live):
    lane = lax.broadcasted_iota(jnp.int32, (ROWS, 128), 1) // KB

    def one(_, carry):
        halves, resid = list(carry[:2]), carry[2]
        for block in range(K // KB):
            at = block // 4
            lanes = slice(at * 128, at * 128 + 128)
            now = halves[at]
            fresh = jnp.maximum(now - resid[:, lanes] * inverse[:, lanes], 0.0)
            if live is not None:
                fresh = fresh * live
            fresh = jnp.where(lane == block % 4, fresh, now)
            change = fresh - now
            if factor != 1.0:
                change = change * factor
            halves[at] = fresh
            both = jnp.concatenate(split(change), axis=1)
            resid = resid + (dot(both, quads[at]) + dot(both, quads[2 + at]))
        return halves[0], halves[1], resid

    first, second, _ = lax.fori_loop(
        0, SWEEPS, one, (state[:, :128], state[:, 128:], resid)
    )
    return jnp.concatenate([first, second], axis=1)


def kernel(
    count_ref, expr_hbm, w_ref, v_ref, h_ref,
    new_w_ref, new_v_ref, new_h_ref,
    expr, ea, eb, et, ma, mb, acc, wp, vp, ht, hb,
    gp, g1, gr, g2, g3, g4, gram,
    dr, pa, pb, ring, qa, qb, cp_, c2, cr, c3, c4, cross,
    rest, rest_in, cross_in, quads,
    local_sem, s1s, s1r, ags, agr, gs, gr_s, hs, hr, rs, rr, qs, qr, zs, zr,
):
    c = lax.axis_index("cell")
    g = lax.axis_index("gene")
    grp = lax.axis_index("grp")
    z, y = c // N, c % N

    def plus(a, k):
        return lax.rem(a + (k + N), N)

    def at_z(k):
        return {"cell": plus(z, k) * N + y}

    def at_y(k):
        return {"cell": z * N + plus(y, k)}

    def at_gene(k):
        return {"gene": lax.rem(g + k, GENES)}

    other = {"grp": 1 - grp}
    started = []

    def send(src, dst, send_sem, recv_sem, device):
        copy = pltpu.make_async_remote_copy(
            src_ref=src, dst_ref=dst, send_sem=send_sem, recv_sem=recv_sem,
            device_id=device, device_id_type=MESH,
        )
        copy.start()
        started.append(copy)
        return copy

    load = pltpu.make_async_copy(expr_hbm, expr, local_sem)
    load.start()

    barrier = pltpu.get_barrier_semaphore()
    for k in range(1, N):
        pl.semaphore_signal(barrier, inc=1, device_id=at_z(k), device_id_type=MESH)
        pl.semaphore_signal(barrier, inc=1, device_id=at_y(k), device_id_type=MESH)
    for k in range(1, GENES):
        pl.semaphore_signal(barrier, inc=1, device_id=at_gene(k), device_id_type=MESH)
    pl.semaphore_signal(barrier, inc=1, device_id=other, device_id_type=MESH)

    wp[...] = jnp.zeros_like(wp)
    vp[...] = jnp.zeros_like(vp)
    wp[0:OWN, :] = w_ref[...]
    vp[0:OWN, :] = v_ref[...]
    mix = (wp[...] + vp[...]).astype(BF16)
    own = vp[...].astype(BF16)
    ht[...] = h_ref[...].T
    ma[z, y] = mix[:HALF]
    mb[y, z] = mix[HALF:]
    gp[...] = dot(mix, mix, 0, 0) + LAMBDA * dot(own, own, 0, 0)

    pl.semaphore_wait(barrier, 2 * (N - 1) + GENES)

    order = [4, 3, 5, 2, 6, 1, 7]
    first = []
    for k in order:
        first.append(send(ma.at[z, y], ma.at[z, y], s1s.at[0, k], s1r.at[0, k], at_y(k)))
        first.append(send(mb.at[y, z], mb.at[y, z], s1s.at[1, k], s1r.at[1, k], at_z(k)))

    def scatter_gene(src, into, row):
        done = []
        for k in range(1, GENES):
            to = lax.rem(g + k, GENES)
            rows = pl.ds(pl.multiple_of(to * ROWS, ROWS), ROWS)
            done.append(send(src.at[rows], into.at[k], gs.at[row, k], gr_s.at[row, k], at_gene(k)))
        return done

    def gather_gene(ref, size, row, sems, sems_r):
        rows = pl.ds(pl.multiple_of(g * size, size), size)
        return [
            send(ref.at[rows], ref.at[rows], sems.at[row, k], sems_r.at[row, k], at_gene(k))
            for k in range(1, GENES)
        ]

    def landed(copies):
        for copy in copies:
            copy.wait_recv()

    my_rows = pl.ds(pl.multiple_of(g * ROWS, ROWS), ROWS)
    my_eight = pl.ds(pl.multiple_of(z * 8, 8), 8)

    def reduce_z(part, into, row):
        done = []
        for k in range(1, N):
            rows = pl.ds(pl.multiple_of(plus(z, k) * 8, 8), 8)
            done.append(send(part.at[rows], into.at[k], zs.at[row, k], zr.at[row, k], at_z(k)))
        return done

    def share_y(part, into, row):
        return [
            send(part, into.at[k], zs.at[row, k], zr.at[row, k], at_y(k)) for k in range(1, N)
        ]

    def gather_z(ref, row):
        return [
            send(
                ref.at[pl.ds(pl.multiple_of(g * ROWS + z * 8, 8), 8)],
                ref.at[pl.ds(pl.multiple_of(g * ROWS + z * 8, 8), 8)],
                zs.at[row, k], zr.at[row, k], at_z(k),
            )
            for k in range(1, N)
        ]

    gram_one = scatter_gene(gp, g1, 0)

    load.wait()

    def lay_out(four, carry):
        part = expr[pl.ds(pl.multiple_of(four * 240, 16), 240), :]
        for k in range(4):
            owner = four * 4 + k
            oz, oy = owner // N, owner % N
            ea[oz, oy] = part[k * OWN : k * OWN + HALF]
            tail = jnp.concatenate(
                [part[k * OWN + HALF : (k + 1) * OWN].astype(F32), jnp.zeros((ROWS - OWN, K), F32)],
                axis=0,
            )
            eb[oy, oz] = tail.astype(BF16)
        return carry

    lax.fori_loop(0, 16, lay_out, 0)

    landed(first)

    ring_ag = {}

    def ag_send(step):
        for sub in range(2):
            for d in (0, 1):
                if step == N // 2 and sub != d:
                    continue
                sign = 1 - 2 * d
                for axis in (0, 1):
                    if step > 1:
                        ring_ag[axis, d, step - 1, sub].wait_recv()
                    if axis == 0:
                        ref = ma.at[plus(z, -sign * (step - 1)), pl.ds(sub * 4, 4)]
                        device = at_z(sign)
                    else:
                        ref = mb.at[plus(y, -sign * (step - 1)), pl.ds(sub * 4, 4)]
                        device = at_y(sign)
                    ring_ag[axis, d, step, sub] = send(
                        ref, ref, ags.at[axis, d, step, sub], agr.at[axis, d, step, sub], device
                    )

    def ag_rest(step):
        for (axis, d, s, sub), copy in ring_ag.items():
            if s == step and (step == N // 2 or (step == N // 2 - 1 and sub != d)):
                copy.wait_recv()

    def chunk_of(ref, index):
        return ref[index].reshape(K, K)

    def drive_part(shifts, fresh=False):
        total = None
        for k in shifts:
            term = dot(chunk_of(et.at[0], plus(z, k)), chunk_of(ma, plus(z, k)))
            term = term + dot(chunk_of(et.at[1], plus(y, k)), chunk_of(mb, plus(y, k)))
            total = term if total is None else total + term
        acc[...] = total if fresh else acc[...] + total

    ag_send(1)

    def turn(k, carry):
        et[0, k] = ea[k].reshape(K, K).T
        et[1, k] = eb[k].reshape(K, K).T
        return carry

    lax.fori_loop(0, N, turn, 0)

    landed(gram_one)
    gr[...] = gp[my_rows, :] + (g1[1] + g1[2] + g1[3])
    gram_two = reduce_z(gr, g2, 0)
    drive_part([0], True)
    ag_send(2)
    landed(gram_two)
    total = gr[my_eight, :]
    for k in range(1, N):
        total = total + g2[k]
    g4[...] = total
    gram_three = share_y(g4, g3, 1)
    drive_part([-1, 1])
    ag_send(3)
    landed(gram_three)
    total = g4[...]
    for k in range(1, N):
        total = total + g3[k]
    gram[pl.ds(pl.multiple_of(g * ROWS + z * 8, 8), 8), :] = total
    gram_four = gather_z(gram, 2)
    drive_part([-2, 2])
    ag_send(4)
    landed(gram_four)
    gram_five = gather_gene(gram, ROWS, 1, gs, gr_s)
    ag_rest(3)
    drive_part([-3, 3])
    ag_rest(4)
    drive_part([4])
    drive_out = scatter_gene(acc, dr, 2)

    landed(gram_five)

    def stage_quad(quad):
        high, low = split(quad)
        for half in (0, 1):
            lanes = slice(half * 128, half * 128 + 128)
            for k in (0, 1):
                rows = slice(k * 128, k * 128 + 128)
                quads[half, rows, :] = high[lanes]
                quads[2 + half, rows, :] = low[lanes]
        return high, low

    state = ht[my_rows, :]
    high, low = stage_quad(gram[...])
    inverse = 1.0 / (block_scale(gram[...]) + TINY)
    resid = dot_split(state, high, low)
    slot = c * K + g * ROWS + lax.broadcasted_iota(jnp.int32, (ROWS, 128), 0)
    live = jnp.where(slot < count_ref[0], 1.0, 0.0).astype(F32)
    landed(drive_out)
    resid = resid - (acc[my_rows, :] + (dr[1] + dr[2] + dr[3]))
    state = sweeps(state, resid, quads, inverse, 1.0, live)
    ht[my_rows, :] = state
    hb[my_rows, :] = state.astype(BF16)
    hb_out = gather_gene(hb, ROWS, 0, hs, hr)
    h_out = gather_gene(ht, ROWS, 1, hs, hr)
    landed(hb_out)

    rings = {}

    def project(k):
        zk, yk = plus(z, k), plus(y, k)
        pa[zk] = dot(chunk_of(ea, zk), hb[...]).reshape(N, HALF, K)
        pb[yk] = dot(chunk_of(eb, yk), hb[...]).reshape(N, HALF, K)

    def rs_send(step):
        for sub in range(2):
            part = pl.ds(sub * 4, 4)
            for d in (0, 1):
                if step == 1 and sub != d:
                    continue
                sign = 1 - 2 * d
                for axis in (0, 1):
                    to = sign * (N // 2 + 1 - step)
                    if axis == 0:
                        mine, device = pa.at[plus(z, to), part], at_z(sign)
                    else:
                        mine, device = pb.at[plus(y, to), part], at_y(sign)
                    if step > 1 and (axis, d, step - 1, sub) in rings:
                        rings[axis, d, step - 1, sub].wait_recv()
                        here = ring.at[axis, d, step - 1, part]
                        here[...] = here[...] + mine[...]
                        mine = here
                    rings[axis, d, step, sub] = send(
                        mine, ring.at[axis, d, step, part],
                        rs.at[axis, d, step, sub], rr.at[axis, d, step, sub], device,
                    )

    project(4)
    rs_send(1)
    cp_[...] = dot(hb[...], hb[...], 0, 0)
    cr[...] = cp_[my_rows, :]
    cross_two = reduce_z(cr, c2, 3)
    project(3)
    project(-3)
    rs_send(2)
    landed(cross_two)
    total = cr[my_eight, :]
    for k in range(1, N):
        total = total + c2[k]
    c4[...] = total
    cross_three = share_y(c4, c3, 4)
    project(2)
    project(-2)
    rs_send(3)
    landed(cross_three)
    total = c4[...]
    for k in range(1, N):
        total = total + c3[k]
    cross[pl.ds(pl.multiple_of(g * ROWS + z * 8, 8), 8), :] = total
    cross_four = gather_z(cross, 5)
    project(1)
    project(-1)
    rs_send(4)
    landed(cross_four)
    cross_five = gather_gene(cross, ROWS, 3, gs, gr_s)
    project(0)
    landed(h_out)
    new_h_ref[...] = ht[...].T
    landed(cross_five)
    cross_other = send(cross, cross_in, gs.at[4, 0], gr_s.at[4, 0], other)
    high, low = stage_quad(cross[...])
    scale = block_scale(cross[...])
    resid = dot_split((1.0 + LAMBDA) * vp[...] + wp[...], high, low)
    for sub in range(2):
        part = pl.ds(sub * 4, 4)
        for axis in (0, 1):
            for d in (0, 1):
                rings[axis, d, 4, sub].wait_recv()
            mine = pa.at[z, part] if axis == 0 else pb.at[y, part]
            mine[...] = mine[...] + (ring[axis, 0, 4, part] + ring[axis, 1, 4, part])
    last = []
    for k in order:
        last.append(send(pa.at[z, plus(y, k)], qa.at[k], qs.at[0, k], qr.at[0, k], at_y(k)))
        last.append(send(pb.at[y, plus(z, k)], qb.at[k], qs.at[1, k], qr.at[1, k], at_z(k)))
    landed(last)
    one, two = pa[z, y], pb[y, z]
    for k in range(1, N):
        one = one + qa[k]
        two = two + qb[k]
    proj = jnp.concatenate([one, two], axis=0)

    state = sweeps(
        vp[...], resid - proj, quads, 1.0 / ((1.0 + LAMBDA) * scale + TINY), 1.0 + LAMBDA, None
    )
    vp[...] = state
    rest[...] = proj - dot_split(state, high, low)
    rest_other = send(rest, rest_in, gs.at[4, 1], gr_s.at[4, 1], other)
    new_v_ref[...] = vp[0:OWN, :]
    landed([cross_other])
    both = cross[...] + cross_in[...]
    high, low = stage_quad(both)
    scale = block_scale(both)
    resid = dot_split(wp[...], high, low)
    landed([rest_other])
    resid = resid - (rest[...] + rest_in[...])
    wp[...] = sweeps(wp[...], resid, quads, 1.0 / (scale + TINY), 1.0, None)
    new_w_ref[...] = wp[0:OWN, :]
    for copy in started:
        copy.wait_send()


def shards(data, shared_w, specific_v, factor_h, cell_count):
    vmem = pl.BlockSpec(memory_space=pltpu.VMEM)
    sems = pltpu.SemaphoreType.DMA
    new_w, new_v, new_h = pl.pallas_call(
        kernel,
        out_shape=(
            jax.ShapeDtypeStruct((OWN, K), F32),
            jax.ShapeDtypeStruct((OWN, K), F32),
            jax.ShapeDtypeStruct((K, K), F32),
        ),
        in_specs=[
            pl.BlockSpec(memory_space=pltpu.SMEM),
            pl.BlockSpec(memory_space=pl.ANY),
            vmem, vmem, vmem,
        ],
        out_specs=(vmem, vmem, vmem),
        scratch_shapes=[
            pltpu.VMEM((N * N * OWN, K), BF16),
            pltpu.VMEM((N, N, HALF, K), BF16),
            pltpu.VMEM((N, N, HALF, K), BF16),
            pltpu.VMEM((2, N, K, K), BF16),
            pltpu.VMEM((N, N, HALF, K), BF16),
            pltpu.VMEM((N, N, HALF, K), BF16),
            pltpu.VMEM((K, K), F32),
            pltpu.VMEM((ROWS, K), F32),
            pltpu.VMEM((ROWS, K), F32),
            pltpu.VMEM((K, K), F32),
            pltpu.VMEM((K, K), BF16),
            pltpu.VMEM((K, K), F32),
            pltpu.VMEM((GENES, ROWS, K), F32),
            pltpu.VMEM((ROWS, K), F32),
            pltpu.VMEM((N, 8, K), F32),
            pltpu.VMEM((N, 8, K), F32),
            pltpu.VMEM((8, K), F32),
            pltpu.VMEM((K, K), F32),
            pltpu.VMEM((GENES, ROWS, K), F32),
            pltpu.VMEM((N, N, HALF, K), F32),
            pltpu.VMEM((N, N, HALF, K), F32),
            pltpu.VMEM((2, 2, 5, N, HALF, K), F32),
            pltpu.VMEM((N, HALF, K), F32),
            pltpu.VMEM((N, HALF, K), F32),
            pltpu.VMEM((K, K), F32),
            pltpu.VMEM((N, 8, K), F32),
            pltpu.VMEM((ROWS, K), F32),
            pltpu.VMEM((N, 8, K), F32),
            pltpu.VMEM((8, K), F32),
            pltpu.VMEM((K, K), F32),
            pltpu.VMEM((ROWS, K), F32),
            pltpu.VMEM((ROWS, K), F32),
            pltpu.VMEM((K, K), F32),
            pltpu.VMEM((4, K, K), BF16),
            sems,
            sems((2, N)), sems((2, N)),
            sems((2, 2, 5, 2)), sems((2, 2, 5, 2)),
            sems((5, GENES)), sems((5, GENES)),
            sems((2, GENES)), sems((2, GENES)),
            sems((2, 2, 5, 2)), sems((2, 2, 5, 2)),
            sems((2, N)), sems((2, N)),
            sems((6, N)), sems((6, N)),
        ],
        compiler_params=pltpu.CompilerParams(
            collective_id=0, has_side_effects=True, vmem_limit_bytes=48 << 20
        ),
        cost_estimate=pl.CostEstimate(
            flops=1200000000, bytes_accessed=4000000, transcendentals=0
        ),
    )(cell_count, data[0], shared_w, specific_v[0], factor_h[0])
    return new_w, new_v[None], new_h[None]


def solution(mesh):
    in_specs = (
        P("grp", "gene", "cell"),
        P(("gene", "cell"), None),
        P("grp", ("gene", "cell"), None),
        P("grp", None, "cell"),
        P("grp"),
    )
    out_specs = (
        P(("gene", "cell"), None),
        P("grp", ("gene", "cell"), None),
        P("grp", None, "cell"),
    )
    return jax.shard_map(shards, mesh=mesh, in_specs=in_specs, out_specs=out_specs, check_vma=False)
```
